32 devices in a mesh: gz: 16 (over z, y, core), row: 2 (over x).
Axes of the slice: x: 2, y: 2, z: 4, core: 2. Of those that a mesh axis runs over, the one named last changes fastest.
Arguments:
- axial_vel: float32 [1024, 256, 256], P('gz', 'row'), may hold values from -6 to 6
- radial_vel: float32 [1024, 256, 256], P('gz', 'row'), may hold values from -6 to 6
- swirl_vel: float32 [1024, 256, 256], P('gz', 'row'), may hold values from -6 to 6
- inflow_rate: float32 [48], replicated, may hold values from 0.25 to 2
- canopy_gore: int32 [1024, 256, 256], P('gz', 'row'), may hold values from 0 to 48, as said below
Outputs:
- axial_out: float32 [1024, 256, 256], P('gz', 'row')
- radial_projected_velocity: float32 [1024, 256, 256], P('gz', 'row')
- swirl_out: float32 [1024, 256, 256], P('gz', 'row')
The draws below stay inside these ranges and needn't reach their ends.
Inputs may be any that keep to these rules, and one draw needn't show every extreme that they name: `canopy_gore`: a canopy cell in azimuthal column t holds gore floor(t * 48 / 256); other cells hold 48.
All inputs are finite; a program needn't handle non-finite values.
Results may differ from the reference program's by a relative error of at most 0.0009.
Values sent between devices are 32-bit elements; how exact they have to be, the bound alone decides.
A program may use at most 128 MiB of HBM per device.

```python
import math
import jax
import jax.numpy as jnp
from jax import lax

NX = 1024
NR = 256
NT = 256
GORES = 48


def draw_canopy_gore(key, part):
    cover = jax.random.randint(key, (NX, NR, NT), 0, 4)
    column = jnp.arange(NT, dtype=jnp.int32) * GORES // NT
    column = jnp.broadcast_to(column[None, None, :], (NX, NR, NT))
    return jnp.where(cover == 0, column, GORES).astype(jnp.int32)


def block_levels(rng, dims, cuts, least, largest):
    gain = 1.0
    for position, parts in cuts:
        heights = jax.random.uniform(jax.random.fold_in(jax.random.fold_in(rng, 6), position), (parts,), jnp.float32, least / len(cuts), largest / len(cuts))
        gain = gain * jnp.repeat(jnp.exp(heights), dims[position] // parts).reshape((-1,) + (1,) * (len(dims) - 1 - position))
    return gain


def normal_values(key, dims, deviation, bound, pieces=(), held_as=jnp.bfloat16):
    values = deviation * jax.random.normal(key, dims, jnp.float32)
    if pieces:
        values = values * block_levels(key, dims, pieces, -0.22, 0.18)
    return jnp.clip(values, -bound, bound).astype(held_as)


def setup_inputs(seed: int = 0) -> dict:
    splits = jax.random.split(jax.random.key(seed), 6)
    axial_vel = normal_values(splits[0], (NX, NR, NT), 1.0, 6.0, ((0, 16), (1, 2)), jnp.float32)
    radial_vel = normal_values(splits[1], (NX, NR, NT), 1.0, 6.0, ((0, 16), (1, 2)), jnp.float32)
    swirl_vel = normal_values(splits[2], (NX, NR, NT), 1.0, 6.0, ((0, 16), (1, 2)), jnp.float32)
    inflow_rate = jnp.clip(jnp.exp(jax.random.uniform(splits[3], (GORES,), jnp.float32, math.log(0.25), math.log(2.0))), 0.25, 2.0)
    canopy_gore = draw_canopy_gore(jax.random.fold_in(splits[5], 71), 0)
    return dict(axial_vel=axial_vel, radial_vel=radial_vel, swirl_vel=swirl_vel, inflow_rate=inflow_rate, canopy_gore=canopy_gore)


helmholtz_shift = 0.001
maximal_precision = lax.Precision.HIGHEST

def azimuth_basis(extent, mode_ids):
    positions = jnp.arange(extent, dtype=jnp.int32)
    half_way = extent // 2
    frequency = jnp.where(mode_ids <= half_way, mode_ids, mode_ids - half_way)
    phases = positions[:, None] * frequency[None, :] % extent
    angles = phases.astype(jnp.float32) * (2.0 * math.pi / extent)
    weights = jnp.where((mode_ids == 0) | (mode_ids == half_way), math.sqrt(1.0 / extent), math.sqrt(2.0 / extent)).astype(jnp.float32)
    return jnp.where((mode_ids > half_way)[None, :], jnp.sin(angles), jnp.cos(angles)) * weights[None, :]

def azimuth_eigen(mode_ids):
    half_way = NT // 2
    frequency = jnp.where(mode_ids <= half_way, mode_ids, mode_ids - half_way)
    angles = frequency.astype(jnp.float32) * (2.0 * math.pi / NT)
    arc_step = 0.75 * NR * 2.0 * math.pi / NT
    return (2.0 - 2.0 * jnp.cos(angles)) / (arc_step * arc_step)

def axial_basis(extent):
    indices = jnp.arange(extent, dtype=jnp.int32) + 1
    phases = indices[:, None] * indices[None, :] % (2 * (extent + 1))
    angles = phases.astype(jnp.float32) * (math.pi / (extent + 1))
    return jnp.sin(angles) * math.sqrt(2.0 / (extent + 1))

def axial_eigen(extent):
    indices = jnp.arange(extent, dtype=jnp.int32) + 1
    return 2.0 - 2.0 * jnp.cos(indices.astype(jnp.float32) * (math.pi / (extent + 1)))

def radial_basis(extent):
    mode_ids = jnp.arange(extent, dtype=jnp.int32)[:, None]
    cell_ids = jnp.arange(extent, dtype=jnp.int32)[None, :]
    phases = mode_ids * (2 * cell_ids + 1) % (4 * extent)
    angles = phases.astype(jnp.float32) * (math.pi / (2 * extent))
    weights = jnp.where(mode_ids == 0, math.sqrt(1.0 / extent), math.sqrt(2.0 / extent)).astype(jnp.float32)
    return jnp.cos(angles) * weights

def radial_eigen(mode_ids):
    return 2.0 - 2.0 * jnp.cos(mode_ids.astype(jnp.float32) * (math.pi / NR))

def cell_radius(cell_ids):
    return cell_ids.astype(jnp.float32) + (0.25 * NR + 0.5)

def reference(axial_vel, radial_vel, swirl_vel, inflow_rate, canopy_gore):
    spacing = 2.0 * math.pi / NT
    radius = cell_radius(jnp.arange(NR, dtype=jnp.int32))[None, :, None]
    axial_pad = jnp.pad(axial_vel, ((1, 1), (0, 0), (0, 0)))
    radial_flux = jnp.pad(radial_vel * radius, ((0, 0), (1, 1), (0, 0)))
    divergence = 0.5 * (axial_pad[2:] - axial_pad[:-2])
    divergence = divergence + (radial_flux[:, 2:] - radial_flux[:, :-2]) / (2.0 * radius)
    divergence = divergence + (jnp.roll(swirl_vel, -1, 2) - jnp.roll(swirl_vel, 1, 2)) / (2.0 * radius * spacing)
    rate_table = jnp.concatenate([inflow_rate, jnp.zeros((1,), jnp.float32)])
    right_side = divergence - jnp.take(rate_table, canopy_gore)
    all_modes = jnp.arange(NT, dtype=jnp.int32)
    fourier = azimuth_basis(NT, all_modes)
    axial_lookup_table = axial_basis(NX)
    radial_table = radial_basis(NR)
    spectrum = jnp.einsum('ijt,tm->mij', right_side, fourier, precision=maximal_precision)
    spectrum = jnp.einsum('ki,mij->mkj', axial_lookup_table, spectrum, precision=maximal_precision)
    spectrum = jnp.einsum('sj,mkj->mks', radial_table, spectrum, precision=maximal_precision)
    denominator = azimuth_eigen(all_modes)[:, None, None] + axial_eigen(NX)[None, :, None]
    denominator = denominator + radial_eigen(jnp.arange(NR, dtype=jnp.int32))[None, None, :] + helmholtz_shift
    scaled = spectrum / denominator
    scaled = jnp.einsum('sj,mks->mkj', radial_table, scaled, precision=maximal_precision)
    scaled = jnp.einsum('ki,mkj->mij', axial_lookup_table, scaled, precision=maximal_precision)
    pressure = -jnp.einsum('mij,tm->ijt', scaled, fourier, precision=maximal_precision)
    axial_p = jnp.pad(pressure, ((1, 1), (0, 0), (0, 0)))
    radial_p = jnp.pad(pressure, ((0, 0), (1, 1), (0, 0)), mode='edge')
    axial_out = axial_vel - 0.5 * (axial_p[2:] - axial_p[:-2])
    radial_projected_velocity = radial_vel - 0.5 * (radial_p[:, 2:] - radial_p[:, :-2])
    swirl_out = swirl_vel - (jnp.roll(pressure, -1, 2) - jnp.roll(pressure, 1, 2)) / (2.0 * radius * spacing)
    return (axial_out, radial_projected_velocity, swirl_out)
```

```python
import functools
import math

import jax
import jax.numpy as jnp
import ml_dtypes
import numpy as np
from jax import lax
from jax.experimental import pallas as pl
from jax.experimental.pallas import tpu as pltpu
from jax.sharding import PartitionSpec as P


SHIFT = 0.001
GORES = 48
XB = 8
F32 = jnp.float32
BF16 = jnp.bfloat16
NN = (((1,), (0,)), ((), ()))
NT_ = (((1,), (1,)), ((), ()))
MIB = 1024 * 1024


def np_split(table):
    high = table.astype(np.float32).astype(ml_dtypes.bfloat16)
    low = (table - high.astype(np.float64)).astype(np.float32).astype(ml_dtypes.bfloat16)
    return high, low


@functools.lru_cache(maxsize=None)
def tables(nx, nr, nt, x_each):
    half = nr // 2
    modes = np.arange(nt)
    freq = np.where(modes <= nt // 2, modes, modes - nt // 2)
    angle = 2 * np.pi * ((np.arange(nt)[None, :] * freq[:, None]) % nt) / nt
    weight = np.where((modes == 0) | (modes == nt // 2), math.sqrt(1 / nt), math.sqrt(2 / nt))
    azimuth = np.where((modes > nt // 2)[:, None], np.sin(angle), np.cos(angle)) * weight[:, None]
    arc = 0.75 * nr * 2 * np.pi / nt
    az = (2 - 2 * np.cos(2 * np.pi * freq / nt)) / arc**2
    s = np.arange(half)
    v = np.where(s == 0, math.sqrt(1 / half), math.sqrt(2 / half))
    radial = np.cos(np.pi * (s[None, :] * (2 * s[:, None] + 1) % (4 * half)) / (2 * half)) * v[None]
    edge = radial[0]
    ra = 2 - 2 * np.cos(np.pi * s / half)
    lam = az[:, None] + ra[None, :] + SHIFT
    t = lam / 2
    r = 1 / (1 + t + np.sqrt(lam + t * t))
    k = np.arange(nx) + 1
    axial = math.sqrt(2 / (nx + 1)) * np.sin(
        np.pi * ((k[:, None] * k[None, :]) % (2 * (nx + 1))) / (nx + 1)
    )
    ax = 2 - 2 * np.cos(np.pi * k / (nx + 1))
    couple = np.zeros((nt, nx))
    for m in range(nt):
        couple[m] = (2 * edge[:, None] ** 2 / (ax[None, :] + lam[m][:, None])).sum(0)
    jump = 1 / (1 + couple)
    power = r**x_each
    kappa = r * (1 - power**2) / (1 - r * r)
    total = r * (1 - r ** (2 * nx)) / (1 - r * r)
    image = r / (1 + r * total)
    thin = np.stack([power, kappa, image], axis=1)
    return dict(
        azimuth=np_split(azimuth),
        radial=np_split(radial),
        radial_flip=np_split(radial[::-1].copy()),
        axial=np_split(axial),
        edge=edge.astype(np.float32)[None],
        r=r.astype(np.float32),
        logr=np.log(r).astype(np.float32),
        rr=(1 / (1 - r * r)).astype(np.float32),
        jump=jump.astype(np.float32),
        thin=thin.astype(np.float32),
    )


def split(x):
    high = x.astype(BF16)
    return high, (x - high.astype(F32)).astype(BF16)


def dot3(a, b, dims):
    dot = functools.partial(lax.dot_general, dimension_numbers=dims, preferred_element_type=F32)
    return dot(a[0], b[0]) + (dot(a[0], b[1]) + dot(a[1], b[0]))


def forward_kernel(
    ax, axp, axn, lo, hi, rv, sw, go, gup, gdn, rate, rad, hinv, sinv, ch, cl, sh, sl, r, e,
    y_out, send, ysc, yc,
):
    step = pl.program_id(0)
    steps = pl.num_programs(0)
    nt = ax.shape[2]
    x_each = ysc.shape[0]

    @pl.when(step == 0)
    def _():
        yc[...] = jnp.zeros_like(yc)

    first, last = step == 0, step == steps - 1
    cc = (ch[...], cl[...])
    ss = (sh[...], sl[...])
    for x in range(XB):
        before = ax[x - 1] if x > 0 else jnp.where(first, lo[0], axp[0])
        after = ax[x + 1] if x < XB - 1 else jnp.where(last, hi[0], axn[0])
        flux = rv[x] * rad[...]
        above = jnp.concatenate([flux[1:], gup[x : x + 1]], axis=0)
        below = jnp.concatenate([gdn[x : x + 1], flux[:-1]], axis=0)
        swirl = sw[x]
        right = 0.5 * (after - before) + (above - below) * hinv[...]
        right = right + (pltpu.roll(swirl, nt - 1, 1) - pltpu.roll(swirl, 1, 1)) * sinv[...]
        right = right - jnp.where(go[x] < GORES, rate[...], 0.0)
        part = dot3(cc, split(right), NT_)
        part = dot3(split(part), ss, NN)
        y = r[...] * (part + yc[...])
        yc[...] = y
        y_out[x] = y
        ysc[step * XB + x] = y

    @pl.when(last)
    def _():
        half = r.shape[1]
        send[:, :half] = yc[...]
        yc[...] = jnp.zeros_like(yc)
        send[:, 2 * half :] = jnp.zeros_like(yc)
        lane = lax.broadcasted_iota(jnp.int32, yc.shape, 1)

        def back(n, carry):
            i = x_each - 1 - n
            p = ysc[i] + r[...] * yc[...]
            yc[...] = p
            g = jnp.sum(p * e[...], axis=1, keepdims=True)
            send[:, 2 * half :] = jnp.where(lane == i, g, send[:, 2 * half :])
            return carry

        lax.fori_loop(0, x_each, back, 0)
        send[:, half : 2 * half] = yc[...]


def thin_kernel(recv, coef, const, e, jump, xh, xl, out, left, gsc, hsc, esc):
    blocks, _, own, _ = recv.shape
    half = e.shape[1]
    x_each = coef.shape[1]
    power, kappa, image = const[:, 0], const[:, 1], const[:, 2]

    def scan(forward, backward):
        def run(start):
            inlet = [start]
            for b in range(blocks - 1):
                inlet.append(forward(b) + power * inlet[-1])
            outlet = [None] * blocks
            outlet[-1] = jnp.zeros_like(start)
            for b in range(blocks - 1, -1, -1):
                value = backward(b) + inlet[b] * kappa + power * outlet[b]
                if b:
                    outlet[b - 1] = value
            return inlet, outlet, value

        value = run(jnp.zeros_like(power))[2]
        return run(-image * value)[:2]

    for row in range(2):
        inlet, outlet = scan(
            lambda b: recv[b, row, :, :half], lambda b: recv[b, row, :, half : 2 * half]
        )
        for b in range(blocks):
            out[b, row, :, :half] = inlet[b]
            out[b, row, :, half : 2 * half] = outlet[b]
    for b in range(blocks):
        left[b, :, :half] = (out[b, 0, :, :half] - out[b, 1, :, :half]) * e[...]
        left[b, :, half:] = (
            out[b, 0, :, half : 2 * half] - out[b, 1, :, half : 2 * half]
        ) * e[...]
    for m in range(own):
        value = dot3(split(left[:, m, :]), split(coef[m]), NT_)
        gsc[:, m, :] = value
    total = None
    for b in range(blocks):
        g = gsc[b] + (
            recv[b, 0, :, 2 * half : 2 * half + x_each]
            - recv[b, 1, :, 2 * half : 2 * half + x_each]
        )
        rows = slice(b * x_each, (b + 1) * x_each)
        term = dot3(split(g), (xh[rows, :], xl[rows, :]), NN)
        total = term if total is None else total + term
    h = dot3(split(total * jump[...]), (xh[...], xl[...]), NN)
    for b in range(blocks):
        hsc[b] = h[:, b * x_each : (b + 1) * x_each]
    for m in range(own):
        value = dot3(split(hsc[:, m, :]), split(coef[m]), NN)
        esc[:, m, :] = value
    inlet, outlet = scan(lambda b: esc[b, :, half:] * e[...], lambda b: esc[b, :, :half] * e[...])
    for b in range(blocks):
        for row, sign in ((0, -1.0), (1, 1.0)):
            out[b, row, :, :half] += sign * inlet[b]
            out[b, row, :, half : 2 * half] += sign * outlet[b]
            out[b, row, :, 2 * half :] = jnp.zeros((own, half), F32)
            out[b, row, :, 2 * half : 2 * half + x_each] = hsc[b]


def backward_kernel(
    y_hbm, recv, ax, rv, sw, dup, ddn, hsw, ch, cl, sh, sl, r, e,
    ax_out, rv_out, sw_out, ysc, pressure, pc, sem,
):
    step = pl.program_id(0)
    steps = pl.num_programs(0)
    half = r.shape[1]
    nt = ax.shape[2]
    x_each = ysc.shape[0] - 1
    cc = (ch[...], cl[...])
    ss = (sh[...], sl[...])

    def inverse(p):
        return dot3(split(dot3(ss, split(p), NT_)), cc, NN)

    def fetch(c):
        return pltpu.make_async_copy(
            y_hbm.at[pl.ds(c * XB, XB)], ysc.at[pl.ds(1 + c * XB, XB)], sem.at[c]
        )

    @pl.when(step == 0)
    def _():
        for c in range(x_each // XB):
            fetch(c).start()
        ysc[0] = recv[:, :half]
        pc[...] = recv[:, :half]
        lane = lax.broadcasted_iota(jnp.int32, pc.shape, 1)
        for c in range(x_each // XB):
            fetch(c).wait()

            def ahead(n, carry):
                i = c * XB + n
                h = jnp.sum(
                    jnp.where(lane == i, recv[:, 2 * half :], 0.0), axis=1, keepdims=True
                )
                z = r[...] * (pc[...] + h * e[...])
                pc[...] = z
                ysc[1 + i] += z
                return carry

            lax.fori_loop(0, XB, ahead, 0)
        outlet = recv[:, half : 2 * half]
        pressure[XB + 1] = inverse(outlet)
        p = ysc[x_each] + r[...] * outlet
        pc[...] = p
        pressure[XB] = inverse(p)

    @pl.when(step > 0)
    def _():
        pressure[XB] = pressure[0]
        pressure[XB + 1] = pressure[1]

    block = steps - 1 - step
    for d in range(XB):
        p = ysc[block * XB + XB - 1 - d] + r[...] * pc[...]
        pc[...] = p
        pressure[XB - 1 - d] = inverse(p)
    for x in range(XB):
        here = pressure[x + 1]
        ax_out[x] = ax[x] + 0.5 * (pressure[x + 2] - pressure[x])
        above = jnp.concatenate([here[1:], here[-1:] + dup[x : x + 1]], axis=0)
        below = jnp.concatenate([here[:1] + ddn[x : x + 1], here[:-1]], axis=0)
        rv_out[x] = rv[x] + 0.5 * (above - below)
        sw_out[x] = sw[x] + (pltpu.roll(here, nt - 1, 1) - pltpu.roll(here, 1, 1)) * hsw[...]


def body(axial_vel, radial_vel, swirl_vel, inflow_rate, canopy_gore):
    x_each, half, nt = axial_vel.shape
    blocks = lax.axis_size("gz")
    rows = lax.axis_size("row")
    assert rows == 2
    nx, nr = x_each * blocks, half * rows
    count = blocks * rows
    own = nt // count
    tab = tables(nx, nr, nt, x_each)
    row = lax.axis_index("row")
    me = lax.axis_index("gz") * rows + row
    top = row == 0
    spacing = 2.0 * math.pi / nt
    ids = row * half + jnp.arange(half, dtype=jnp.int32)
    radius = jnp.broadcast_to((ids.astype(F32) + (0.25 * nr + 0.5))[:, None], (half, nt))
    hinv = 0.5 / radius
    sinv = 0.5 / (radius * spacing)
    up = [(i, i + 1) for i in range(blocks - 1)]
    down = [(i + 1, i) for i in range(blocks - 1)]
    lo = lax.ppermute(axial_vel[-1:], "gz", up)
    hi = lax.ppermute(axial_vel[:1], "gz", down)
    edge = jnp.where(top, radial_vel[:, half - 1], radial_vel[:, 0])
    ghost = lax.ppermute(edge, "row", [(0, 1), (1, 0)])
    gup = jnp.where(top, ghost * (0.25 * nr + 0.5 + half), 0.0)
    gdn = jnp.where(top, 0.0, ghost * (0.25 * nr - 0.5 + half))
    column = np.arange(nt) * GORES // nt
    hot = (column[:, None] == np.arange(GORES)[None, :]).astype(np.float32)
    rate = jnp.sum(jnp.where(hot > 0, inflow_rate[None, :], 0.0), axis=1)[None, :]
    ch, cl = (jnp.asarray(a) for a in tab["azimuth"])
    sh, sl = (jnp.where(top, a, b) for a, b in zip(tab["radial_flip"], tab["radial"]))
    r = jnp.asarray(tab["r"])
    e = jnp.asarray(tab["edge"])
    steps = x_each // XB
    width = 3 * half

    def whole(*shape):
        return pl.BlockSpec(shape, lambda i: (0,) * len(shape))

    block = pl.BlockSpec((XB, half, nt), lambda i: (i, 0, 0))
    line = pl.BlockSpec((XB, nt), lambda i: (i, 0))
    y, send = pl.pallas_call(
        forward_kernel,
        grid=(steps,),
        in_specs=[
            block,
            pl.BlockSpec((1, half, nt), lambda i: (jnp.maximum(i * XB - 1, 0), 0, 0)),
            pl.BlockSpec((1, half, nt), lambda i: (jnp.minimum(i * XB + XB, x_each - 1), 0, 0)),
            whole(1, half, nt), whole(1, half, nt),
            block, block, block, line, line,
            whole(1, nt), whole(half, nt), whole(half, nt), whole(half, nt),
            whole(nt, nt), whole(nt, nt), whole(half, half), whole(half, half),
            whole(nt, half), whole(1, half),
        ],
        out_specs=[pl.BlockSpec((XB, nt, half), lambda i: (i, 0, 0)), whole(nt, width)],
        out_shape=[
            jax.ShapeDtypeStruct((x_each, nt, half), F32),
            jax.ShapeDtypeStruct((nt, width), F32),
        ],
        scratch_shapes=[pltpu.VMEM((x_each, nt, half), F32), pltpu.VMEM((nt, half), F32)],
        compiler_params=pltpu.CompilerParams(vmem_limit_bytes=48 * MIB),
        name="forward",
    )(
        axial_vel, axial_vel, axial_vel, lo, hi, radial_vel, swirl_vel, canopy_gore, gup, gdn,
        rate, radius, hinv, sinv, ch, cl, sh, sl, r, e,
    )

    recv = lax.all_to_all(send, ("gz", "row"), split_axis=0, concat_axis=0, tiled=True)
    recv = recv.reshape(blocks, rows, own, width)

    def mine(table):
        return lax.dynamic_slice_in_dim(jnp.asarray(table), me * own, own, 0)

    place = jnp.arange(x_each, dtype=F32)[None, :, None]
    logr = mine(tab["logr"])[:, None, :]
    near = jnp.exp(logr * (place + 1)) * (1 - jnp.exp(logr * (2 * x_each - 2 * place)))
    coef = jnp.concatenate(
        [near * mine(tab["rr"])[:, None, :], jnp.exp(logr * (x_each - place))], axis=2
    )
    vm = pl.BlockSpec(memory_space=pltpu.VMEM)
    answer = pl.pallas_call(
        thin_kernel,
        in_specs=[vm] * 7,
        out_specs=vm,
        out_shape=jax.ShapeDtypeStruct((blocks, rows, own, width), F32),
        scratch_shapes=[
            pltpu.VMEM((blocks, own, 2 * half), F32),
            pltpu.VMEM((blocks, own, x_each), F32),
            pltpu.VMEM((blocks, own, x_each), F32),
            pltpu.VMEM((blocks, own, 2 * half), F32),
        ],
        compiler_params=pltpu.CompilerParams(vmem_limit_bytes=48 * MIB),
        name="thin",
    )(recv, coef, mine(tab["thin"]), e, mine(tab["jump"]), *(jnp.asarray(a) for a in tab["axial"]))

    back = lax.all_to_all(
        answer.reshape(nt, width), ("gz", "row"), split_axis=0, concat_axis=0, tiled=True
    )
    jump = jnp.einsum(
        "mi,mt->it",
        back[:, 2 * half : 2 * half + x_each],
        ch.astype(F32) + cl.astype(F32),
        precision=lax.Precision.HIGHEST,
    )
    dup = jnp.where(top, -jump, 0.0)
    ddn = jnp.where(top, 0.0, jump)
    block = pl.BlockSpec((XB, half, nt), lambda i: (steps - 1 - i, 0, 0))
    line = pl.BlockSpec((XB, nt), lambda i: (steps - 1 - i, 0))
    shape = jax.ShapeDtypeStruct(axial_vel.shape, F32)
    return pl.pallas_call(
        backward_kernel,
        grid=(steps,),
        in_specs=[
            pl.BlockSpec(memory_space=pl.ANY), whole(nt, width), block, block, block, line, line,
            whole(half, nt), whole(nt, nt), whole(nt, nt), whole(half, half), whole(half, half),
            whole(nt, half), whole(1, half),
        ],
        out_specs=[block, block, block],
        out_shape=[shape, shape, shape],
        scratch_shapes=[
            pltpu.VMEM((x_each + 1, nt, half), F32),
            pltpu.VMEM((XB + 2, half, nt), F32),
            pltpu.VMEM((nt, half), F32),
            pltpu.SemaphoreType.DMA((steps,)),
        ],
        compiler_params=pltpu.CompilerParams(vmem_limit_bytes=48 * MIB),
        name="backward",
    )(
        y, back, axial_vel, radial_vel, swirl_vel, dup, ddn, sinv, ch, cl, sh, sl, r,
        jnp.where(top, -e, e),
    )


def solution(mesh):
    placed = P("gz", "row", None)
    return jax.shard_map(
        body,
        mesh=mesh,
        in_specs=(placed, placed, placed, P(), placed),
        out_specs=(placed, placed, placed),
        check_vma=False,
    )
```

```python
import functools
import math

import jax
import jax.numpy as jnp
import ml_dtypes
import numpy as np
from jax import lax
from jax.experimental import pallas as pl
from jax.experimental.pallas import tpu as pltpu
from jax.sharding import PartitionSpec as P


SHIFT = 0.001
GORES = 48
XB = 8
F32 = jnp.float32
BF16 = jnp.bfloat16
NN = (((1,), (0,)), ((), ()))
NT_ = (((1,), (1,)), ((), ()))
MIB = 1024 * 1024


def np_split(table):
    high = table.astype(np.float32).astype(ml_dtypes.bfloat16)
    low = (table - high.astype(np.float64)).astype(np.float32).astype(ml_dtypes.bfloat16)
    return high, low


@functools.lru_cache(maxsize=None)
def tables(nx, nr, nt, x_each):
    half = nr // 2
    modes = np.arange(nt)
    freq = np.where(modes <= nt // 2, modes, modes - nt // 2)
    angle = 2 * np.pi * ((np.arange(nt)[None, :] * freq[:, None]) % nt) / nt
    weight = np.where((modes == 0) | (modes == nt // 2), math.sqrt(1 / nt), math.sqrt(2 / nt))
    azimuth = np.where((modes > nt // 2)[:, None], np.sin(angle), np.cos(angle)) * weight[:, None]
    arc = 0.75 * nr * 2 * np.pi / nt
    az = (2 - 2 * np.cos(2 * np.pi * freq / nt)) / arc**2
    s = np.arange(half)
    v = np.where(s == 0, math.sqrt(1 / half), math.sqrt(2 / half))
    radial = np.cos(np.pi * (s[None, :] * (2 * s[:, None] + 1) % (4 * half)) / (2 * half)) * v[None]
    edge = radial[0]
    ra = 2 - 2 * np.cos(np.pi * s / half)
    lam = az[:, None] + ra[None, :] + SHIFT
    t = lam / 2
    r = 1 / (1 + t + np.sqrt(lam + t * t))
    k = np.arange(nx) + 1
    axial = math.sqrt(2 / (nx + 1)) * np.sin(
        np.pi * ((k[:, None] * k[None, :]) % (2 * (nx + 1))) / (nx + 1)
    )
    ax = 2 - 2 * np.cos(np.pi * k / (nx + 1))
    couple = np.zeros((nt, nx))
    for m in range(nt):
        couple[m] = (2 * edge[:, None] ** 2 / (ax[None, :] + lam[m][:, None])).sum(0)
    jump = 1 / (1 + couple)
    power = r**x_each
    kappa = r * (1 - power**2) / (1 - r * r)
    total = r * (1 - r ** (2 * nx)) / (1 - r * r)
    image = r / (1 + r * total)
    thin = np.stack([power, kappa, image], axis=1)
    return dict(
        azimuth=np_split(azimuth),
        flat=(azimuth * radial[0, 0]).astype(np.float32),
        radial=np_split(radial),
        radial_flip=np_split(radial[::-1].copy()),
        axial=np_split(axial),
        edge=edge.astype(np.float32)[None],
        r=r.astype(np.float32),
        logr=np.log(r).astype(np.float32),
        rr=(1 / (1 - r * r)).astype(np.float32),
        jump=jump.astype(np.float32),
        thin=thin.astype(np.float32),
    )


def split(x):
    high = x.astype(BF16)
    return high, (x - high.astype(F32)).astype(BF16)


def dot3(a, b, dims):
    dot = functools.partial(lax.dot_general, dimension_numbers=dims, preferred_element_type=F32)
    return dot(a[0], b[0]) + (dot(a[0], b[1]) + dot(a[1], b[0]))


def forward_kernel(
    ax, axp, axn, lo, hi, rv, sw, go, gup, gdn, rate, rad, hinv, sinv, ch, cl, sh, sl, r, e,
    y_out, send, ysc, yc,
):
    step = pl.program_id(0)
    steps = pl.num_programs(0)
    nt = ax.shape[2]
    x_each = ysc.shape[0]

    @pl.when(step == 0)
    def _():
        yc[...] = jnp.zeros_like(yc)

    first, last = step == 0, step == steps - 1
    cc = (ch[...], cl[...])
    ss = (sh[...], sl[...])
    for x in range(XB):
        before = ax[x - 1] if x > 0 else jnp.where(first, lo[0], axp[0])
        after = ax[x + 1] if x < XB - 1 else jnp.where(last, hi[0], axn[0])
        flux = rv[x] * rad[...]
        above = jnp.concatenate([flux[1:], gup[x : x + 1]], axis=0)
        below = jnp.concatenate([gdn[x : x + 1], flux[:-1]], axis=0)
        swirl = sw[x]
        right = 0.5 * (after - before) + (above - below) * hinv[...]
        right = right + (pltpu.roll(swirl, nt - 1, 1) - pltpu.roll(swirl, 1, 1)) * sinv[...]
        right = right - jnp.where(go[x] < GORES, rate[...], 0.0)
        part = dot3(cc, split(right), NT_)
        part = dot3(split(part), ss, NN)
        y = r[...] * (part + yc[...])
        yc[...] = y
        y_out[x] = y
        ysc[step * XB + x] = y

    @pl.when(last)
    def _():
        half = r.shape[1]
        send[:, :half] = yc[...]
        yc[...] = jnp.zeros_like(yc)
        send[:, 2 * half :] = jnp.zeros_like(yc)
        lane = lax.broadcasted_iota(jnp.int32, yc.shape, 1)

        def back(n, carry):
            i = x_each - 1 - n
            p = ysc[i] + r[...] * yc[...]
            yc[...] = p
            g = jnp.sum(p * e[...], axis=1, keepdims=True)
            send[:, 2 * half :] = jnp.where(lane == i, g, send[:, 2 * half :])
            return carry

        lax.fori_loop(0, x_each, back, 0)
        send[:, half : 2 * half] = yc[...]


def thin_kernel(recv, coef, const, e, jump, xh, xl, out, left, gsc, hsc, esc):
    blocks, _, own, _ = recv.shape
    half = e.shape[1]
    x_each = coef.shape[1]
    power, kappa, image = const[:, 0], const[:, 1], const[:, 2]

    def scan(forward, backward):
        def run(start):
            inlet = [start]
            for b in range(blocks - 1):
                inlet.append(forward(b) + power * inlet[-1])
            outlet = [None] * blocks
            outlet[-1] = jnp.zeros_like(start)
            for b in range(blocks - 1, -1, -1):
                value = backward(b) + inlet[b] * kappa + power * outlet[b]
                if b:
                    outlet[b - 1] = value
            return inlet, outlet, value

        value = run(jnp.zeros_like(power))[2]
        return run(-image * value)[:2]

    for row in range(2):
        inlet, outlet = scan(
            lambda b: recv[b, row, :, :half], lambda b: recv[b, row, :, half : 2 * half]
        )
        for b in range(blocks):
            out[b, row, :, :half] = inlet[b]
            out[b, row, :, half : 2 * half] = outlet[b]
    for b in range(blocks):
        left[b, :, :half] = (out[b, 0, :, :half] - out[b, 1, :, :half]) * e[...]
        left[b, :, half:] = (
            out[b, 0, :, half : 2 * half] - out[b, 1, :, half : 2 * half]
        ) * e[...]
    for m in range(own):
        value = dot3(split(left[:, m, :]), split(coef[m]), NT_)
        gsc[:, m, :] = value
    total = None
    for b in range(blocks):
        g = gsc[b] + (
            recv[b, 0, :, 2 * half : 2 * half + x_each]
            - recv[b, 1, :, 2 * half : 2 * half + x_each]
        )
        rows = slice(b * x_each, (b + 1) * x_each)
        term = dot3(split(g), (xh[rows, :], xl[rows, :]), NN)
        total = term if total is None else total + term
    h = dot3(split(total * jump[...]), (xh[...], xl[...]), NN)
    for b in range(blocks):
        hsc[b] = h[:, b * x_each : (b + 1) * x_each]
    for m in range(own):
        value = dot3(split(hsc[:, m, :]), split(coef[m]), NN)
        esc[:, m, :] = value
    inlet, outlet = scan(lambda b: esc[b, :, half:] * e[...], lambda b: esc[b, :, :half] * e[...])
    for b in range(blocks):
        for row, sign in ((0, -1.0), (1, 1.0)):
            out[b, row, :, :half] += sign * inlet[b]
            out[b, row, :, half : 2 * half] += sign * outlet[b]
            out[b, row, :, 2 * half :] = jnp.zeros((own, half), F32)
            out[b, row, :, 2 * half : 2 * half + x_each] = hsc[b]


def backward_kernel(
    y_hbm, recv, ax, rv, sw, dup, ddn, hsw, ch, cl, cf, sh, sl, r, e,
    ax_out, rv_out, sw_out, ysc, pressure, pc, sem,
):
    step = pl.program_id(0)
    steps = pl.num_programs(0)
    half = r.shape[1]
    nt = ax.shape[2]
    x_each = ysc.shape[0] - 1
    cc = (ch[...], cl[...])
    ss = (sh[...], sl[...])

    def inverse(p):
        flat = jnp.sum(p[:, :1] * cf[...], axis=0, keepdims=True)
        rest = jnp.where(lax.broadcasted_iota(jnp.int32, p.shape, 1) == 0, 0.0, p)
        return dot3(split(dot3(ss, split(rest), NT_)), cc, NN) + flat

    def fetch(c):
        return pltpu.make_async_copy(
            y_hbm.at[pl.ds(c * XB, XB)], ysc.at[pl.ds(1 + c * XB, XB)], sem.at[c]
        )

    @pl.when(step == 0)
    def _():
        for c in range(x_each // XB):
            fetch(c).start()
        ysc[0] = recv[:, :half]
        pc[...] = recv[:, :half]
        lane = lax.broadcasted_iota(jnp.int32, pc.shape, 1)
        for c in range(x_each // XB):
            fetch(c).wait()

            def ahead(n, carry):
                i = c * XB + n
                h = jnp.sum(
                    jnp.where(lane == i, recv[:, 2 * half :], 0.0), axis=1, keepdims=True
                )
                z = r[...] * (pc[...] + h * e[...])
                pc[...] = z
                ysc[1 + i] += z
                return carry

            lax.fori_loop(0, XB, ahead, 0)
        outlet = recv[:, half : 2 * half]
        pressure[XB + 1] = inverse(outlet)
        p = ysc[x_each] + r[...] * outlet
        pc[...] = p
        pressure[XB] = inverse(p)

    @pl.when(step > 0)
    def _():
        pressure[XB] = pressure[0]
        pressure[XB + 1] = pressure[1]

    block = steps - 1 - step
    for d in range(XB):
        p = ysc[block * XB + XB - 1 - d] + r[...] * pc[...]
        pc[...] = p
        pressure[XB - 1 - d] = inverse(p)
    for x in range(XB):
        here = pressure[x + 1]
        ax_out[x] = ax[x] + 0.5 * (pressure[x + 2] - pressure[x])
        above = jnp.concatenate([here[1:], here[-1:] + dup[x : x + 1]], axis=0)
        below = jnp.concatenate([here[:1] + ddn[x : x + 1], here[:-1]], axis=0)
        rv_out[x] = rv[x] + 0.5 * (above - below)
        sw_out[x] = sw[x] + (pltpu.roll(here, nt - 1, 1) - pltpu.roll(here, 1, 1)) * hsw[...]


def body(axial_vel, radial_vel, swirl_vel, inflow_rate, canopy_gore):
    x_each, half, nt = axial_vel.shape
    blocks = lax.axis_size("gz")
    rows = lax.axis_size("row")
    assert rows == 2
    nx, nr = x_each * blocks, half * rows
    count = blocks * rows
    own = nt // count
    tab = tables(nx, nr, nt, x_each)
    row = lax.axis_index("row")
    me = lax.axis_index("gz") * rows + row
    top = row == 0
    spacing = 2.0 * math.pi / nt
    ids = row * half + jnp.arange(half, dtype=jnp.int32)
    radius = jnp.broadcast_to((ids.astype(F32) + (0.25 * nr + 0.5))[:, None], (half, nt))
    hinv = 0.5 / radius
    sinv = 0.5 / (radius * spacing)
    up = [(i, i + 1) for i in range(blocks - 1)]
    down = [(i + 1, i) for i in range(blocks - 1)]
    lo = lax.ppermute(axial_vel[-1:], "gz", up)
    hi = lax.ppermute(axial_vel[:1], "gz", down)
    edge = jnp.where(top, radial_vel[:, half - 1], radial_vel[:, 0])
    ghost = lax.ppermute(edge, "row", [(0, 1), (1, 0)])
    gup = jnp.where(top, ghost * (0.25 * nr + 0.5 + half), 0.0)
    gdn = jnp.where(top, 0.0, ghost * (0.25 * nr - 0.5 + half))
    column = np.arange(nt) * GORES // nt
    hot = (column[:, None] == np.arange(GORES)[None, :]).astype(np.float32)
    rate = jnp.sum(jnp.where(hot > 0, inflow_rate[None, :], 0.0), axis=1)[None, :]
    ch, cl = (jnp.asarray(a) for a in tab["azimuth"])
    sh, sl = (jnp.where(top, a, b) for a, b in zip(tab["radial_flip"], tab["radial"]))
    r = jnp.asarray(tab["r"])
    e = jnp.asarray(tab["edge"])
    steps = x_each // XB
    width = 3 * half

    def whole(*shape):
        return pl.BlockSpec(shape, lambda i: (0,) * len(shape))

    block = pl.BlockSpec((XB, half, nt), lambda i: (i, 0, 0))
    line = pl.BlockSpec((XB, nt), lambda i: (i, 0))
    y, send = pl.pallas_call(
        forward_kernel,
        grid=(steps,),
        in_specs=[
            block,
            pl.BlockSpec((1, half, nt), lambda i: (jnp.maximum(i * XB - 1, 0), 0, 0)),
            pl.BlockSpec((1, half, nt), lambda i: (jnp.minimum(i * XB + XB, x_each - 1), 0, 0)),
            whole(1, half, nt), whole(1, half, nt),
            block, block, block, line, line,
            whole(1, nt), whole(half, nt), whole(half, nt), whole(half, nt),
            whole(nt, nt), whole(nt, nt), whole(half, half), whole(half, half),
            whole(nt, half), whole(1, half),
        ],
        out_specs=[pl.BlockSpec((XB, nt, half), lambda i: (i, 0, 0)), whole(nt, width)],
        out_shape=[
            jax.ShapeDtypeStruct((x_each, nt, half), F32),
            jax.ShapeDtypeStruct((nt, width), F32),
        ],
        scratch_shapes=[pltpu.VMEM((x_each, nt, half), F32), pltpu.VMEM((nt, half), F32)],
        compiler_params=pltpu.CompilerParams(vmem_limit_bytes=48 * MIB),
        name="forward",
    )(
        axial_vel, axial_vel, axial_vel, lo, hi, radial_vel, swirl_vel, canopy_gore, gup, gdn,
        rate, radius, hinv, sinv, ch, cl, sh, sl, r, e,
    )

    recv = lax.all_to_all(send, ("gz", "row"), split_axis=0, concat_axis=0, tiled=True)
    recv = recv.reshape(blocks, rows, own, width)

    def mine(table):
        return lax.dynamic_slice_in_dim(jnp.asarray(table), me * own, own, 0)

    place = jnp.arange(x_each, dtype=F32)[None, :, None]
    logr = mine(tab["logr"])[:, None, :]
    near = jnp.exp(logr * (place + 1)) * (1 - jnp.exp(logr * (2 * x_each - 2 * place)))
    coef = jnp.concatenate(
        [near * mine(tab["rr"])[:, None, :], jnp.exp(logr * (x_each - place))], axis=2
    )
    vm = pl.BlockSpec(memory_space=pltpu.VMEM)
    answer = pl.pallas_call(
        thin_kernel,
        in_specs=[vm] * 7,
        out_specs=vm,
        out_shape=jax.ShapeDtypeStruct((blocks, rows, own, width), F32),
        scratch_shapes=[
            pltpu.VMEM((blocks, own, 2 * half), F32),
            pltpu.VMEM((blocks, own, x_each), F32),
            pltpu.VMEM((blocks, own, x_each), F32),
            pltpu.VMEM((blocks, own, 2 * half), F32),
        ],
        compiler_params=pltpu.CompilerParams(vmem_limit_bytes=48 * MIB),
        name="thin",
    )(recv, coef, mine(tab["thin"]), e, mine(tab["jump"]), *(jnp.asarray(a) for a in tab["axial"]))

    back = lax.all_to_all(
        answer.reshape(nt, width), ("gz", "row"), split_axis=0, concat_axis=0, tiled=True
    )
    jump = jnp.einsum(
        "mi,mt->it",
        back[:, 2 * half : 2 * half + x_each],
        ch.astype(F32) + cl.astype(F32),
        precision=lax.Precision.HIGHEST,
    )
    dup = jnp.where(top, -jump, 0.0)
    ddn = jnp.where(top, 0.0, jump)
    block = pl.BlockSpec((XB, half, nt), lambda i: (steps - 1 - i, 0, 0))
    line = pl.BlockSpec((XB, nt), lambda i: (steps - 1 - i, 0))
    shape = jax.ShapeDtypeStruct(axial_vel.shape, F32)
    return pl.pallas_call(
        backward_kernel,
        grid=(steps,),
        in_specs=[
            pl.BlockSpec(memory_space=pl.ANY), whole(nt, width), block, block, block, line, line,
            whole(half, nt), whole(nt, nt), whole(nt, nt), whole(nt, nt), whole(half, half),
            whole(half, half), whole(nt, half), whole(1, half),
        ],
        out_specs=[block, block, block],
        out_shape=[shape, shape, shape],
        scratch_shapes=[
            pltpu.VMEM((x_each + 1, nt, half), F32),
            pltpu.VMEM((XB + 2, half, nt), F32),
            pltpu.VMEM((nt, half), F32),
            pltpu.SemaphoreType.DMA((steps,)),
        ],
        compiler_params=pltpu.CompilerParams(vmem_limit_bytes=48 * MIB),
        name="backward",
    )(
        y, back, axial_vel, radial_vel, swirl_vel, dup, ddn, sinv, ch, cl, jnp.asarray(tab["flat"]), sh, sl, r,
        jnp.where(top, -e, e),
    )


def solution(mesh):
    placed = P("gz", "row", None)
    return jax.shard_map(
        body,
        mesh=mesh,
        in_specs=(placed, placed, placed, P(), placed),
        out_specs=(placed, placed, placed),
        check_vma=False,
    )
```
